32 devices in a mesh: blk: 16 (over z, x, core), fiber: 2 (over y).
Axes of the slice: x: 2, y: 2, z: 4, core: 2. Of those that a mesh axis runs over, the one named last changes fastest.
Arguments:
- queries: bfloat16 [8192, 256], P(('blk', 'fiber')), may hold values from -6 to 6
- keys: bfloat16 [8192, 256], P(('blk', 'fiber')), may hold values from -6 to 6
- values: bfloat16 [8192, 256], P(('blk', 'fiber')), may hold values from -6 to 6
- tiles: int32 [16, 2, 4, 4], P('blk', 'fiber'), may hold values from -1 to 7, as said below
- edges: bfloat16 [16, 2, 4, 4, 128, 128], P('blk', 'fiber'), may hold values from 0.05 to 2, as said below
Outputs:
- attended: bfloat16 [8192, 256], P(('blk', 'fiber'))
The draws below stay inside these ranges and needn't reach their ends.
Inputs may be any that keep to these rules, and one draw needn't show every extreme that they name: tiles[b, f, s, :] lists the occupied tiles between query block b and key subblock f of block (b - s) mod 16: distinct numbers r * 2 + c (row tile r, column tile c) in the first slots, then -1 in the slots left over. Each list holds at least one tile, and in every draw some list is full. edges[c, f, s, k] holds the edge values of the tile in slot k of the list tiles[(c + s) mod 16, f, s]; slots marked -1 there hold values of no edge.
All inputs are finite; a program needn't handle non-finite values.
Results may differ from the reference program's by a relative error of at most 0.0049.
Values may be sent and summed in bfloat16 or wider, within the bound.
No kernel may reach another device: no remote copies, remote signals or barrier semaphores. Data moves between devices by JAX's collectives and lax.ppermute only.
A program may use at most 128 MiB of HBM per device.

```python
import jax
import jax.numpy as jnp
from jax import lax

F = 256
HEADS = 4
TILE = 128
KS = 256
STOPS = 4
DH = 64
BLOCKS = 16
FIBERS = 2
ROWS = 512
NODES = 8192
TILES_PAIR = 8
CAP = 4
N_FIBER = 2


def draw_tiles(key, part):
    list_count = BLOCKS * FIBERS * STOPS
    list_keys = jax.random.split(jax.random.fold_in(key, 11), list_count)
    shuffled = jax.vmap(lambda single: jax.random.permutation(single, TILES_PAIR))(list_keys)[:, :CAP]
    counts = jax.random.randint(jax.random.fold_in(key, 12), (list_count,), 1, CAP + 1)
    chosen = jax.random.randint(jax.random.fold_in(key, 13), (), 0, list_count)
    counts = jnp.where(jnp.arange(list_count) == chosen, CAP, counts)
    slot_ids = jnp.where(jnp.arange(CAP)[None, :] < counts[:, None], shuffled, -1)
    return slot_ids.reshape(BLOCKS, FIBERS, STOPS, CAP).astype(jnp.int32)


def draw_edges(key, part):
    shape = (BLOCKS, FIBERS, STOPS, CAP, TILE, TILE)
    drawn = jax.random.uniform(jax.random.fold_in(key, 23), shape, jnp.float32, 0.1, 1.5)
    return drawn.astype(jnp.bfloat16)


def levels(rng, shape, shards, low, high):
    gain, own = 1.0, jax.random.fold_in(rng, 6)
    for axis_at, shards_of in shards:
        heights = jnp.exp(jax.random.uniform(jax.random.fold_in(own, axis_at), (shards_of,), jnp.float32, low / len(shards), high / len(shards)))
        gain = gain * jnp.repeat(heights, shape[axis_at] // shards_of).reshape([-1 if axis == axis_at else 1 for axis in range(len(shape))])
    return gain


def normal_values(stream_key, extent, scale, reach, cuts=(), kind=jnp.bfloat16):
    values = scale * jax.random.normal(stream_key, extent, jnp.float32)
    if cuts:
        values = values * levels(stream_key, extent, cuts, -0.22, 0.18)
    return jnp.clip(values, -reach, reach).astype(kind)


def setup_inputs(seed: int = 0) -> dict:
    arg_keys = jax.random.split(jax.random.key(seed), 6)
    queries = normal_values(arg_keys[0], (NODES, F), 1.0, 6.0, ((0, 32),))
    keys = normal_values(arg_keys[1], (NODES, F), 1.0, 6.0, ((0, 32),))
    values = normal_values(arg_keys[2], (NODES, F), 1.0, 6.0, ((0, 32),))
    tiles = draw_tiles(jax.random.fold_in(arg_keys[5], 71), 0)
    edges = draw_edges(jax.random.fold_in(arg_keys[5], 71), 0)
    return {"queries": queries, "keys": keys, "values": values, "tiles": tiles, "edges": edges}


LEAKY_SLOPE = 0.2

def reference(queries, keys, values, tiles, edges):
    row_tiles = ROWS // TILE
    key_tiles = KS // TILE
    score_scale = DH ** (-0.5)
    edge_scale = (STOPS * N_FIBER * KS / 4) ** (-0.5)
    highest = lax.Precision.HIGHEST
    query_blocks = queries.reshape(BLOCKS, row_tiles, TILE, F)
    key_blocks = keys.reshape(BLOCKS, FIBERS, key_tiles, TILE, F)
    value_blocks = values.reshape(BLOCKS, FIBERS, key_tiles, TILE, F)

    def per_block(block_index):
        query_tiles = query_blocks[block_index]

        def one_list(running, combo_index):
            numerator, denominator = running
            fiber_index = combo_index // STOPS
            stop_index = combo_index % STOPS
            owner_block = (block_index - stop_index + BLOCKS) % BLOCKS
            slot_ids = tiles[block_index, fiber_index, stop_index]
            in_use = slot_ids >= 0
            safe_ids = jnp.where(in_use, slot_ids, 0).astype(jnp.int32)
            row_tile = (safe_ids // key_tiles).astype(jnp.int32)
            col_tile = (safe_ids % key_tiles).astype(jnp.int32)
            query_sel = query_tiles[row_tile].astype(jnp.float32).reshape(CAP, TILE, HEADS, DH)
            key_sel = key_blocks[owner_block, fiber_index][col_tile].astype(jnp.float32).reshape(CAP, TILE, HEADS, DH)
            value_sel = value_blocks[owner_block, fiber_index][col_tile].astype(jnp.float32).reshape(CAP, TILE, HEADS, DH)
            scores = jnp.einsum('gqhd,gkhd->ghqk', query_sel, key_sel, precision=highest) * score_scale
            slot_edges = edges[owner_block, fiber_index, stop_index].astype(jnp.float32)
            weights = jnp.where(scores > 0, scores, LEAKY_SLOPE * scores) * slot_edges[:, None] * edge_scale
            weights = weights * in_use[:, None, None, None].astype(jnp.float32)
            squares = lax.optimization_barrier(jnp.sum(weights * weights, axis=3))
            denominator = denominator + jax.ops.segment_sum(squares, row_tile, num_segments=row_tiles)
            rounded = lax.optimization_barrier(weights.astype(jnp.bfloat16)).astype(jnp.float32)
            blended = jnp.einsum('ghqk,gkhd->gqhd', rounded, value_sel, precision=highest).reshape(CAP, TILE, F)
            numerator = numerator + jax.ops.segment_sum(blended, row_tile, num_segments=row_tiles)
            return ((numerator, denominator), None)
        start_pair = (jnp.zeros((row_tiles, TILE, F), jnp.float32), jnp.zeros((row_tiles, HEADS, TILE), jnp.float32))
        (numerator, denominator), _ = lax.scan(one_list, start_pair, jnp.arange(FIBERS * STOPS, dtype=jnp.int32))
        spread = jnp.sqrt(1.0 + jnp.transpose(denominator, (0, 2, 1)))
        result = numerator.reshape(row_tiles, TILE, HEADS, DH) / spread[..., None]
        return result.reshape(ROWS, F).astype(jnp.bfloat16)
    blocks_out = lax.map(per_block, jnp.arange(BLOCKS, dtype=jnp.int32))
    return blocks_out.reshape(NODES, F)
```

```python
import functools
import math

import jax
import jax.numpy as jnp
from jax import lax
from jax.experimental import pallas as pl
from jax.experimental.pallas import tpu as pltpu
from jax.sharding import PartitionSpec as P

HEADS = 4
LEAKY_SLOPE = 0.2
CORES = 2
UNROLL = 4
EXTRA_ROWS = 16
LANES = 128
VMEM_BYTES = 24 * 2**20


def moved(block, axis, distance):
    count = lax.axis_size(axis)
    return lax.ppermute(block, axis, [((i - distance) % count, i) for i in range(count)])


def routed(block, source_of):
    count = lax.axis_size("blk")
    return lax.ppermute(block, "blk", [(source_of(i) % count, i) for i in range(count)])


def head_masked(block, head_count):
    head_dim = block.shape[1] // head_count
    head_of = lax.broadcasted_iota(jnp.int32, block.shape, 1) // head_dim
    return jnp.concatenate(
        [jnp.where(head_of == h, block, jnp.zeros_like(block)) for h in range(head_count)], axis=0
    )


def attend_kernel(tiles_ref, *refs, stop_ids, fibers, key_tiles, tile, head_count, scale):
    stops = len(stop_ids)
    queries = refs[:fibers]
    blocks = refs[fibers : fibers + 3 * stops]
    num_ref, den_ref = refs[fibers + 3 * stops : fibers + 3 * stops + 2]
    payload_ref = refs[fibers + 3 * stops + 2]
    query_ref, sums_ref, squares_ref = refs[fibers + 3 * stops + 3 :]
    rows, feats = queries[0].shape
    capacity = tiles_ref.shape[-1]
    group = math.gcd(capacity, UNROLL)
    fiber = lax.axis_index("fiber")
    core = lax.rem(lax.axis_index("blk"), CORES)
    for r in range(fibers):
        query_ref[r * rows : (r + 1) * rows, :] = queries[r][...]
    sums_ref[...] = jnp.zeros_like(sums_ref)
    squares_ref[...] = jnp.zeros_like(squares_ref)
    for n, stop_of in enumerate(stop_ids):
        key_ref, value_ref, edge_ref = blocks[3 * n : 3 * n + 3]
        stop = stop_of(core)
        keys = [head_masked(key_ref[c * tile : (c + 1) * tile, :], head_count) for c in range(key_tiles)]
        values = [head_masked(value_ref[c * tile : (c + 1) * tile, :], head_count) for c in range(key_tiles)]

        def one_group(g, carry, keys=keys, values=values, edge_ref=edge_ref, stop=stop):
            for k in range(group):
                slot = g * group + k
                listed = tiles_ref[0, 0, stop, slot]
                used = listed >= 0
                number = jnp.maximum(listed, 0)
                row_tile = lax.div(number, key_tiles)
                col_tile = lax.rem(number, key_tiles)
                part = lax.rem(lax.div(row_tile, key_tiles) - fiber + fibers, fibers)
                at = pl.multiple_of((part * key_tiles + lax.rem(row_tile, key_tiles)) * tile, tile)
                key_stack, value_stack = keys[0], values[0]
                for c in range(1, key_tiles):
                    key_stack = jnp.where(col_tile == c, keys[c], key_stack)
                    value_stack = jnp.where(col_tile == c, values[c], value_stack)
                scores = lax.dot_general(
                    query_ref[pl.ds(at, tile), :],
                    key_stack,
                    (((1,), (1,)), ((), ())),
                    preferred_element_type=jnp.float32,
                )
                edge = jnp.where(used, edge_ref[slot].astype(jnp.float32) * scale, 0.0)
                weights = jnp.maximum(scores, LEAKY_SLOPE * scores) * jnp.concatenate([edge] * head_count, axis=1)
                squares_ref[pl.ds(at, tile), :] += weights * weights
                sums_ref[pl.ds(at, tile), :] += jnp.dot(
                    weights.astype(jnp.bfloat16), value_stack, preferred_element_type=jnp.float32
                )
            return carry

        if capacity == group:
            one_group(0, 0)
        else:
            lax.fori_loop(0, capacity // group, one_group, 0)

    lane = lax.broadcasted_iota(jnp.int32, (tile, LANES), 1)

    def totals(at):
        den = jnp.zeros((tile, LANES), jnp.float32)
        for h in range(head_count):
            total = jnp.sum(squares_ref[at : at + tile, h * tile : (h + 1) * tile], axis=1, keepdims=True)
            den = jnp.where(lane == h, total, den)
        return den

    num_ref[...] = sums_ref[:rows, :]
    for t in range(key_tiles):
        den_ref[t * tile : (t + 1) * tile, :] = totals(t * tile)
    for r in range(1, fibers):
        payload_ref[r - 1, :rows, :] = sums_ref[r * rows : (r + 1) * rows, :].astype(jnp.bfloat16)
        for t in range(key_tiles):
            den = totals(r * rows + t * tile)
            high = den.astype(jnp.bfloat16)
            rest = (den - high.astype(jnp.float32)).astype(jnp.bfloat16)
            half = EXTRA_ROWS // 2
            both = jnp.concatenate(
                [high.astype(jnp.float32).T[:half], rest.astype(jnp.float32).T[:half]], axis=0
            )
            payload_ref[r - 1, rows : rows + EXTRA_ROWS, t * tile : (t + 1) * tile] = both.astype(jnp.bfloat16)


def finish_kernel(num_ref, den_ref, *refs, key_tiles, tile, head_count):
    *payloads, out_ref = refs
    rows, feats = num_ref.shape
    head_dim = feats // head_count
    half = EXTRA_ROWS // 2
    head_of = lax.broadcasted_iota(jnp.int32, (tile, feats), 1) // head_dim
    for t in range(key_tiles):
        here = slice(t * tile, (t + 1) * tile)
        num = num_ref[here, :]
        den = den_ref[here, :]
        for payload in payloads:
            num = num + payload[here, :].astype(jnp.float32)
            both = payload[rows : rows + EXTRA_ROWS, here].astype(jnp.float32)
            total = both[:half] + both[half:]
            padded = jnp.concatenate([total, jnp.zeros((LANES - half, tile), jnp.float32)], axis=0)
            den = den + padded.T
        spread = lax.rsqrt(1.0 + den)
        factor = jnp.broadcast_to(spread[:, 0:1], (tile, feats))
        for h in range(1, head_count):
            factor = jnp.where(head_of == h, spread[:, h : h + 1], factor)
        out_ref[here, :] = (num * factor).astype(jnp.bfloat16)


def on_device(queries, keys, values, tiles, edges):
    fibers = lax.axis_size("fiber")
    rows, feats = keys.shape
    stops, capacity, tile = tiles.shape[2], tiles.shape[3], edges.shape[-1]
    key_tiles = rows // tile
    head_dim = feats // HEADS
    scale = head_dim ** (-0.5) * (stops * fibers * rows / 4) ** (-0.5)
    core = lax.rem(lax.axis_index("blk"), CORES)
    own_edges = edges[0, 0]

    def edges_of(stop):
        return lax.dynamic_index_in_dim(own_edges, stop, 0, keepdims=False)

    blocks = [(keys, values, edges)]
    stop_ids = [lambda core: 0]
    for m in range(1, stops // 2):
        shift = CORES * m
        far_keys, far_values = moved((keys, values), "blk", shift)
        far_edges = moved(own_edges[shift], "blk", shift)
        cross_edges = edges_of(jnp.where(core == 1, shift - 1, shift + 1))
        cross_edges = routed(cross_edges, lambda i, shift=shift: (i - shift) ^ 1)
        near_keys, near_values = routed((far_keys, far_values), lambda i: i ^ 1)
        blocks.append((far_keys, far_values, far_edges))
        stop_ids.append(lambda core, shift=shift: shift)
        blocks.append((near_keys, near_values, cross_edges))
        stop_ids.append(lambda core, shift=shift: jnp.where(core == 0, shift - 1, shift + 1))
    last_edges = edges_of(jnp.where(core == 1, stops - 1, 1))
    blocks.append(
        routed((keys, values, last_edges), lambda i: i - 1 if i % CORES else i - stops + 1)
    )
    stop_ids.append(lambda core: jnp.where(core == 0, stops - 1, 1))
    all_queries = [queries] + [moved(queries, "fiber", -r) for r in range(1, fibers)]

    whole = pl.BlockSpec(memory_space=pltpu.VMEM)
    own_list = pl.BlockSpec((None, None, None, capacity, tile, tile), lambda i: (0, 0, 0, 0, 0, 0))
    num, den, payload = pl.pallas_call(
        functools.partial(
            attend_kernel,
            stop_ids=stop_ids,
            fibers=fibers,
            key_tiles=key_tiles,
            tile=tile,
            head_count=HEADS,
            scale=scale,
        ),
        grid=(1,),
        in_specs=[pl.BlockSpec(memory_space=pltpu.SMEM)]
        + [whole] * fibers
        + [whole, whole, own_list]
        + [whole] * (3 * (stops - 1)),
        out_specs=[whole] * 3,
        out_shape=[
            jax.ShapeDtypeStruct((rows, feats), jnp.float32),
            jax.ShapeDtypeStruct((rows, LANES), jnp.float32),
            jax.ShapeDtypeStruct((max(fibers - 1, 1), rows + EXTRA_ROWS, feats), jnp.bfloat16),
        ],
        scratch_shapes=[
            pltpu.VMEM((fibers * rows, feats), jnp.bfloat16),
            pltpu.VMEM((fibers * rows, feats), jnp.float32),
            pltpu.VMEM((fibers * rows, HEADS * tile), jnp.float32),
        ],
        compiler_params=pltpu.CompilerParams(vmem_limit_bytes=VMEM_BYTES),
    )(tiles, *all_queries, *[part for block in blocks for part in block])
    arrived = [moved(payload[r - 1], "fiber", r) for r in range(1, fibers)]
    return pl.pallas_call(
        functools.partial(finish_kernel, key_tiles=key_tiles, tile=tile, head_count=HEADS),
        in_specs=[whole] * (2 + len(arrived)),
        out_specs=whole,
        out_shape=jax.ShapeDtypeStruct((rows, feats), jnp.bfloat16),
        compiler_params=pltpu.CompilerParams(vmem_limit_bytes=VMEM_BYTES),
    )(num, den, *arrived)


def solution(mesh):
    return jax.shard_map(
        on_device,
        mesh=mesh,
        in_specs=(
            P(("blk", "fiber"), None),
            P(("blk", "fiber"), None),
            P(("blk", "fiber"), None),
            P("blk", "fiber", None, None),
            P("blk", "fiber", None, None, None, None),
        ),
        out_specs=P(("blk", "fiber"), None),
        check_vma=False,
    )
```

```python
import functools
import math

import jax
import jax.numpy as jnp
from jax import lax
from jax.experimental import pallas as pl
from jax.experimental.pallas import tpu as pltpu
from jax.sharding import PartitionSpec as P

HEADS = 4
LEAKY_SLOPE = 0.2
CORES = 2
UNROLL = 4
EXTRA_ROWS = 16
LANES = 128
VMEM_BYTES = 16 * 2**20
WHOLE = pl.BlockSpec(memory_space=pltpu.VMEM)
ANYWHERE = pl.BlockSpec(memory_space=pltpu.HBM)
PARAMS = pltpu.CompilerParams(vmem_limit_bytes=VMEM_BYTES)
SHORT = pl.CostEstimate(flops=1, bytes_accessed=1, transcendentals=0)


def moved(block, axis, distance):
    count = lax.axis_size(axis)
    return lax.ppermute(block, axis, [((i - distance) % count, i) for i in range(count)])


def routed(block, source_of):
    count = lax.axis_size("blk")
    return lax.ppermute(block, "blk", [(source_of(i) % count, i) for i in range(count)])


def core_of_blk():
    return lax.rem(lax.axis_index("blk"), CORES)


def pack_kernel(key_ref, value_ref, edges_ref, *refs, lists):
    *outs, sem = refs
    rows, feats = key_ref.shape
    list_rows = edges_ref.shape[1]
    core = core_of_blk()
    copies = []
    for out_ref, (with_block, stops) in zip(outs, lists):
        at = 0
        if with_block:
            for ref in (key_ref, value_ref):
                for c in range(0, feats, LANES):
                    copies.append((ref.at[:, c : c + LANES], out_ref.at[at : at + rows, :]))
                    at += rows
        for stop in stops:
            copies.append((edges_ref.at[stop(core)], out_ref.at[at : at + list_rows, :]))
            at += list_rows
    running = [pltpu.make_async_copy(a, b, sem.at[n]) for n, (a, b) in enumerate(copies)]
    for copy in running:
        copy.start()
    for copy in running:
        copy.wait()


def packed(keys, values, edges, lists):
    rows, feats = keys.shape
    capacity, tile = edges.shape[3], edges.shape[4]
    block = 2 * feats // LANES
    sizes = [(block * rows if with_block else 0) + len(stops) * capacity * tile for with_block, stops in lists]
    count = sum((block if with_block else 0) + len(stops) for with_block, stops in lists)
    return pl.pallas_call(
        functools.partial(pack_kernel, lists=lists),
        in_specs=[ANYWHERE] * 3,
        out_specs=[WHOLE] * len(lists),
        out_shape=[jax.ShapeDtypeStruct((size, LANES), jnp.bfloat16) for size in sizes],
        scratch_shapes=[pltpu.SemaphoreType.DMA((count,))],
        compiler_params=PARAMS,
        cost_estimate=SHORT,
    )(*[pltpu.with_memory_space_constraint(x, pltpu.HBM) for x in (keys, values, edges.reshape(edges.shape[2], capacity * tile, tile))])


def head_masked(block, head_count):
    head_dim = block.shape[1] // head_count
    head_of = lax.broadcasted_iota(jnp.int32, block.shape, 1) // head_dim
    return jnp.concatenate(
        [jnp.where(head_of == h, block, jnp.zeros_like(block)) for h in range(head_count)], axis=0
    )


def tile_of(part, c, rows, tile, feats):
    ref, at = part
    wide = ref.shape[1]
    starts = [at + piece * rows + c * tile for piece in range(feats // wide)]
    return jnp.concatenate([ref[s : s + tile, :] for s in starts], axis=1)


def add_stop(n, tiles_ref, stop, keys, values, edges, query_ref, sums_ref, squares_ref, stack_ref, sizes):
    fibers, key_tiles, tile, scale = sizes
    capacity = tiles_ref.shape[-1]
    group = math.gcd(capacity, UNROLL)
    fiber = lax.axis_index("fiber")
    tall = HEADS * tile
    lane = lax.broadcasted_iota(jnp.int32, (tile, LANES), 1)
    for c in range(key_tiles):
        stack_ref[2 * n, c * tall : (c + 1) * tall, :] = head_masked(tile_of(keys, c, key_tiles * tile, tile, query_ref.shape[1]), HEADS)
        stack_ref[2 * n + 1, c * tall : (c + 1) * tall, :] = head_masked(tile_of(values, c, key_tiles * tile, tile, query_ref.shape[1]), HEADS)

    def one_group(g, carry):
        for k in range(group):
            slot = g * group + k
            listed = tiles_ref[0, 0, stop, slot]
            number = jnp.maximum(listed, 0)
            row_tile = lax.div(number, key_tiles)
            col_tile = lax.rem(number, key_tiles)
            part = lax.rem(lax.div(row_tile, key_tiles) - fiber + fibers, fibers)
            at = pl.multiple_of((part * key_tiles + lax.rem(row_tile, key_tiles)) * tile, tile)
            stack = pl.ds(pl.multiple_of(col_tile * tall, tall), tall)
            scores = lax.dot_general(
                query_ref[pl.ds(at, tile), :],
                stack_ref[2 * n, stack, :],
                (((1,), (1,)), ((), ())),
                preferred_element_type=jnp.float32,
            )
            edge_rows = pl.ds(edges[1] + slot * tile, tile)
            if not isinstance(slot, int):
                edge_rows = pl.ds(pl.multiple_of(edges[1] + slot * tile, tile), tile)
            edge = jnp.where(listed >= 0, edges[0][edge_rows, :].astype(jnp.float32) * scale, 0.0)
            weights = jnp.maximum(scores, LEAKY_SLOPE * scores) * jnp.concatenate([edge] * HEADS, axis=1)
            squared = weights * weights
            den = jnp.zeros((tile, LANES), jnp.float32)
            for h in range(HEADS):
                total = jnp.sum(squared[:, h * tile : (h + 1) * tile], axis=1, keepdims=True)
                den = jnp.where(lane == h, total, den)
            squares_ref[pl.ds(at, tile), :] += den
            sums_ref[pl.ds(at, tile), :] += jnp.dot(
                weights.astype(jnp.bfloat16), stack_ref[2 * n + 1, stack, :], preferred_element_type=jnp.float32
            )
        return carry

    if capacity == group:
        one_group(0, 0)
    else:
        lax.fori_loop(0, capacity // group, one_group, 0)


def first_kernel(tiles_ref, *refs, plan, packets, sizes):
    fibers, key_tiles, tile, scale = sizes
    queries, arrived = refs[:fibers], refs[fibers : fibers + packets]
    query_ref, sums_ref, squares_ref, stack_ref = refs[fibers + packets :]
    rows = key_tiles * tile
    for r in range(fibers):
        query_ref[r * rows : (r + 1) * rows, :] = queries[r][...]
    sums_ref[...] = jnp.zeros_like(sums_ref)
    squares_ref[...] = jnp.zeros_like(squares_ref)
    add_plan(tiles_ref, plan, arrived, query_ref, sums_ref, squares_ref, stack_ref, sizes)


def add_plan(tiles_ref, plan, arrived, query_ref, sums_ref, squares_ref, stack_ref, sizes):
    core = core_of_blk()
    for n, (stop, *parts) in enumerate(plan):
        parts = [(arrived[packet], at) for packet, at in parts]
        add_stop(n, tiles_ref, stop(core), *parts, query_ref, sums_ref, squares_ref, stack_ref, sizes)


def more_kernel(tiles_ref, query_ref, sums_in, squares_in, *refs, plan, packets, sizes):
    arrived = refs[:packets]
    sums_ref, squares_ref, stack_ref = refs[packets:]
    sums_ref[...] = sums_in[...]
    squares_ref[...] = squares_in[...]
    add_plan(tiles_ref, plan, arrived, query_ref, sums_ref, squares_ref, stack_ref, sizes)


def last_kernel(tiles_ref, query_ref, sums_in, squares_in, *refs, plan, packets, sizes):
    arrived = refs[:packets]
    num_ref, den_ref, payload_ref, stack_ref, sums_ref, squares_ref = refs[packets:]
    sums_ref[...] = sums_in[...]
    squares_ref[...] = squares_in[...]
    add_plan(tiles_ref, plan, arrived, query_ref, sums_ref, squares_ref, stack_ref, sizes)
    hand_out(sums_ref, squares_ref, num_ref, den_ref, payload_ref, sizes)


def hand_out(sums_ref, squares_ref, num_ref, den_ref, payload_ref, sizes):
    fibers, key_tiles, tile, scale = sizes
    rows = key_tiles * tile
    half = EXTRA_ROWS // 2
    for r in range(1, fibers):
        payload_ref[r - 1, :rows, :] = sums_ref[r * rows : (r + 1) * rows, :].astype(jnp.bfloat16)
        for t in range(key_tiles):
            den = squares_ref[r * rows + t * tile : r * rows + (t + 1) * tile, :]
            high = den.astype(jnp.bfloat16)
            rest = den - high.astype(jnp.float32)
            both = jnp.concatenate([high.astype(jnp.float32).T[:half], rest.T[:half]], axis=0)
            payload_ref[r - 1, rows : rows + EXTRA_ROWS, t * tile : (t + 1) * tile] = both.astype(jnp.bfloat16)
    num_ref[...] = sums_ref[:rows, :]
    den_ref[...] = squares_ref[:rows, :]


def finish_kernel(num_ref, den_ref, *refs, sizes):
    fibers, key_tiles, tile, scale = sizes
    *payloads, out_ref = refs
    rows, feats = num_ref.shape
    head_dim = feats // HEADS
    half = EXTRA_ROWS // 2
    head_of = lax.broadcasted_iota(jnp.int32, (tile, feats), 1) // head_dim
    for t in range(key_tiles):
        here = slice(t * tile, (t + 1) * tile)
        num = num_ref[here, :]
        den = den_ref[here, :]
        for payload in payloads:
            num = num + payload[here, :].astype(jnp.float32)
            both = payload[rows : rows + EXTRA_ROWS, here].astype(jnp.float32)
            total = both[:half] + both[half:]
            padded = jnp.concatenate([total, jnp.zeros((LANES - half, tile), jnp.float32)], axis=0)
            den = den + padded.T
        spread = lax.rsqrt(1.0 + den)
        factor = jnp.broadcast_to(spread[:, 0:1], (tile, feats))
        for h in range(1, HEADS):
            factor = jnp.where(head_of == h, spread[:, h : h + 1], factor)
        out_ref[here, :] = (num * factor).astype(jnp.bfloat16)


def on_device(queries, keys, values, tiles, edges):
    fibers = lax.axis_size("fiber")
    rows, feats = keys.shape
    stops, capacity, tile = tiles.shape[2], tiles.shape[3], edges.shape[-1]
    key_tiles = rows // tile
    scale = (feats // HEADS) ** (-0.5) * (stops * fibers * rows / 4) ** (-0.5)
    sizes = (fibers, key_tiles, tile, scale)
    half_rows = feats // LANES * rows
    list_rows = capacity * tile

    shifts = range(CORES, stops, CORES)
    far = [moved((keys, values), "blk", s) for s in shifts]
    own, odd, *pairs = packed(
        keys, values, edges,
        [
            (True, [lambda core: 0]),
            (True, [lambda core: jnp.where(core == 1, stops - 1, 1)]),
        ]
        + [(False, [lambda core, s=s: jnp.where(core == 1, s - 1, s + 1), lambda core, s=s: s]) for s in shifts],
    )
    near = [routed(block, lambda i: i ^ 1) for block in far]
    pairs = [moved(pair, "blk", s) for pair, s in zip(pairs, shifts)]
    odd = routed(odd, lambda i: i - 1 if i % CORES else i - stops + 1)
    all_queries = [queries] + [moved(queries, "fiber", -r) for r in range(1, fibers)]

    smem = pl.BlockSpec(memory_space=pltpu.SMEM)
    state = [
        jax.ShapeDtypeStruct((fibers * rows, feats), jnp.bfloat16),
        jax.ShapeDtypeStruct((fibers * rows, feats), jnp.float32),
        jax.ShapeDtypeStruct((fibers * rows, LANES), jnp.float32),
    ]

    def stack(count):
        return pltpu.VMEM((2 * count, key_tiles * HEADS * tile, feats), jnp.bfloat16)

    plan = [(lambda core: 0, (0, 0), (0, half_rows), (0, 2 * half_rows))]
    all_q, sums, squares = pl.pallas_call(
        functools.partial(first_kernel, plan=plan, packets=1, sizes=sizes),
        in_specs=[smem] + [WHOLE] * (1 + fibers),
        out_specs=[WHOLE] * 3,
        out_shape=state,
        scratch_shapes=[stack(len(plan))],
        compiler_params=PARAMS,
        cost_estimate=SHORT,
    )(tiles, *all_queries, own)
    pairs, near, all_q, sums, squares = lax.optimization_barrier((pairs, near, all_q, sums, squares))
    arrived, plan = [], []
    for s, pair, far_block, near_block in zip(shifts, pairs, far, near):
        at = len(arrived)
        arrived += [*far_block, pair, *near_block, routed(pair, lambda i: i ^ 1)]
        plan.append((lambda core, s=s: s, (at, 0), (at + 1, 0), (at + 2, list_rows)))
        plan.append((lambda core, s=s: jnp.where(core == 0, s - 1, s + 1), (at + 3, 0), (at + 4, 0), (at + 5, 0)))
    sums, squares = pl.pallas_call(
        functools.partial(more_kernel, plan=plan, packets=len(arrived), sizes=sizes),
        in_specs=[smem] + [WHOLE] * (3 + len(arrived)),
        out_specs=[WHOLE] * 2,
        out_shape=state[1:],
        scratch_shapes=[stack(len(plan))],
        compiler_params=PARAMS,
        cost_estimate=SHORT,
    )(tiles, all_q, sums, squares, *arrived)
    arrived = [odd]
    plan = [(lambda core: jnp.where(core == 0, stops - 1, 1), (0, 0), (0, half_rows), (0, 2 * half_rows))]
    num, den, payload = pl.pallas_call(
        functools.partial(last_kernel, plan=plan, packets=len(arrived), sizes=sizes),
        in_specs=[smem] + [WHOLE] * (3 + len(arrived)),
        out_specs=[WHOLE] * 3,
        out_shape=[
            jax.ShapeDtypeStruct((rows, feats), jnp.float32),
            jax.ShapeDtypeStruct((rows, LANES), jnp.float32),
            jax.ShapeDtypeStruct((max(fibers - 1, 1), rows + EXTRA_ROWS, feats), jnp.bfloat16),
        ],
        scratch_shapes=[stack(len(plan)), pltpu.VMEM(state[1].shape, jnp.float32), pltpu.VMEM(state[2].shape, jnp.float32)],
        compiler_params=PARAMS,
        cost_estimate=SHORT,
    )(tiles, all_q, sums, squares, *arrived)
    partials = [moved(payload[r - 1], "fiber", r) for r in range(1, fibers)]
    return pl.pallas_call(
        functools.partial(finish_kernel, sizes=sizes),
        in_specs=[WHOLE] * (2 + len(partials)),
        out_specs=WHOLE,
        out_shape=jax.ShapeDtypeStruct((rows, feats), jnp.bfloat16),
        compiler_params=PARAMS,
        cost_estimate=SHORT,
    )(num, den, *partials)


def solution(mesh):
    return jax.shard_map(
        on_device,
        mesh=mesh,
        in_specs=(
            P(("blk", "fiber"), None),
            P(("blk", "fiber"), None),
            P(("blk", "fiber"), None),
            P("blk", "fiber", None, None),
            P("blk", "fiber", None, None, None, None),
        ),
        out_specs=P(("blk", "fiber"), None),
        check_vma=False,
    )
```

```python
import functools
import math

import jax
import jax.numpy as jnp
from jax import lax
from jax.experimental import pallas as pl
from jax.experimental.pallas import tpu as pltpu
from jax.sharding import PartitionSpec as P

HEADS = 4
LEAKY_SLOPE = 0.2
CORES = 2
UNROLL = 4
EXTRA_ROWS = 16
LANES = 128
VMEM_BYTES = 16 * 2**20
WHOLE = pl.BlockSpec(memory_space=pltpu.VMEM)
ANYWHERE = pl.BlockSpec(memory_space=pltpu.HBM)
PARAMS = pltpu.CompilerParams(vmem_limit_bytes=VMEM_BYTES)
SHORT = pl.CostEstimate(flops=1, bytes_accessed=1, transcendentals=0)


def moved(block, axis, distance):
    count = lax.axis_size(axis)
    return lax.ppermute(block, axis, [((i - distance) % count, i) for i in range(count)])


def routed(block, source_of):
    count = lax.axis_size("blk")
    return lax.ppermute(block, "blk", [(source_of(i) % count, i) for i in range(count)])


def core_of_blk():
    return lax.rem(lax.axis_index("blk"), CORES)


def pack_kernel(key_ref, value_ref, edges_ref, *refs, lists):
    *outs, sem = refs
    rows, feats = key_ref.shape
    list_rows = edges_ref.shape[1]
    core = core_of_blk()
    copies = []
    for out_ref, (with_block, stops) in zip(outs, lists):
        at = 0
        if with_block:
            for ref in (key_ref, value_ref):
                for c in range(0, feats, LANES):
                    copies.append((ref.at[:, c : c + LANES], out_ref.at[at : at + rows, :]))
                    at += rows
        for stop in stops:
            copies.append((edges_ref.at[stop(core)], out_ref.at[at : at + list_rows, :]))
            at += list_rows
    running = [pltpu.make_async_copy(a, b, sem.at[n]) for n, (a, b) in enumerate(copies)]
    for copy in running:
        copy.start()
    for copy in running:
        copy.wait()


def packed(keys, values, edges, lists):
    rows, feats = keys.shape
    capacity, tile = edges.shape[3], edges.shape[4]
    block = 2 * feats // LANES
    sizes = [(block * rows if with_block else 0) + len(stops) * capacity * tile for with_block, stops in lists]
    count = sum((block if with_block else 0) + len(stops) for with_block, stops in lists)
    return pl.pallas_call(
        functools.partial(pack_kernel, lists=lists),
        in_specs=[ANYWHERE] * 3,
        out_specs=[WHOLE] * len(lists),
        out_shape=[jax.ShapeDtypeStruct((size, LANES), jnp.bfloat16) for size in sizes],
        scratch_shapes=[pltpu.SemaphoreType.DMA((count,))],
        compiler_params=PARAMS,
        cost_estimate=SHORT,
    )(*[pltpu.with_memory_space_constraint(x, pltpu.HBM) for x in (keys, values, edges.reshape(edges.shape[2], capacity * tile, tile))])


def head_masked(block, head_count):
    head_dim = block.shape[1] // head_count
    head_of = lax.broadcasted_iota(jnp.int32, block.shape, 1) // head_dim
    return jnp.concatenate(
        [jnp.where(head_of == h, block, jnp.zeros_like(block)) for h in range(head_count)], axis=0
    )


def tile_of(part, c, rows, tile, feats):
    ref, at = part
    wide = ref.shape[1]
    starts = [at + piece * rows + c * tile for piece in range(feats // wide)]
    return jnp.concatenate([ref[s : s + tile, :] for s in starts], axis=1)


def stack_keys(key_stack, at, block):
    feats, tile = block.shape[1], block.shape[0]
    turned = block.T
    head_of = lax.broadcasted_iota(jnp.int32, (feats, tile), 0) // (feats // HEADS)
    key_stack[at] = jnp.concatenate(
        [jnp.where(head_of == h, turned, jnp.zeros_like(turned)) for h in range(HEADS)], axis=1
    )


def stacks(count, key_tiles, tile, feats):
    return [
        pltpu.VMEM((count * key_tiles, feats, HEADS * tile), jnp.bfloat16),
        pltpu.VMEM((count * key_tiles, HEADS * tile, feats), jnp.bfloat16),
    ]


def add_stop(n, tiles_ref, stop, keys, values, edges, query_ref, sums_ref, squares_ref, stack_ref, sizes):
    fibers, key_tiles, tile, scale = sizes
    capacity = tiles_ref.shape[-1]
    group = math.gcd(capacity, UNROLL)
    fiber = lax.axis_index("fiber")
    key_stack, value_stack = stack_ref
    lane = lax.broadcasted_iota(jnp.int32, (tile, LANES), 1)
    for c in range(key_tiles):
        stack_keys(key_stack, n * key_tiles + c, tile_of(keys, c, key_tiles * tile, tile, query_ref.shape[1]))
        value_stack[n * key_tiles + c] = head_masked(tile_of(values, c, key_tiles * tile, tile, query_ref.shape[1]), HEADS)

    def one_group(g, carry):
        for k in range(group):
            slot = g * group + k
            listed = tiles_ref[0, 0, stop, slot]
            number = jnp.maximum(listed, 0)
            row_tile = lax.div(number, key_tiles)
            col_tile = lax.rem(number, key_tiles)
            part = lax.rem(lax.div(row_tile, key_tiles) - fiber + fibers, fibers)
            at = pl.multiple_of((part * key_tiles + lax.rem(row_tile, key_tiles)) * tile, tile)
            scores = jnp.dot(
                query_ref[pl.ds(at, tile), :], key_stack[n * key_tiles + col_tile], preferred_element_type=jnp.float32
            )
            edge_rows = pl.ds(edges[1] + slot * tile, tile)
            if not isinstance(slot, int):
                edge_rows = pl.ds(pl.multiple_of(edges[1] + slot * tile, tile), tile)
            edge = jnp.where(listed >= 0, edges[0][edge_rows, :].astype(jnp.float32) * scale, 0.0)
            weights = jnp.maximum(scores, LEAKY_SLOPE * scores) * jnp.concatenate([edge] * HEADS, axis=1)
            squared = weights * weights
            den = jnp.zeros((tile, LANES), jnp.float32)
            for h in range(HEADS):
                total = jnp.sum(squared[:, h * tile : (h + 1) * tile], axis=1, keepdims=True)
                den = jnp.where(lane == h, total, den)
            squares_ref[pl.ds(at, tile), :] += den
            sums_ref[pl.ds(at, tile), :] += jnp.dot(
                weights.astype(jnp.bfloat16), value_stack[n * key_tiles + col_tile], preferred_element_type=jnp.float32
            )
        return carry

    if capacity == group:
        one_group(0, 0)
    else:
        lax.fori_loop(0, capacity // group, one_group, 0)


def first_kernel(tiles_ref, *refs, plan, packets, sizes):
    fibers, key_tiles, tile, scale = sizes
    queries, arrived = refs[:fibers], refs[fibers : fibers + packets]
    query_ref, sums_ref, squares_ref, *stack_ref = refs[fibers + packets :]
    rows = key_tiles * tile
    for r in range(fibers):
        query_ref[r * rows : (r + 1) * rows, :] = queries[r][...]
    sums_ref[...] = jnp.zeros_like(sums_ref)
    squares_ref[...] = jnp.zeros_like(squares_ref)
    add_plan(tiles_ref, plan, arrived, query_ref, sums_ref, squares_ref, stack_ref, sizes)


def add_plan(tiles_ref, plan, arrived, query_ref, sums_ref, squares_ref, stack_ref, sizes):
    core = core_of_blk()
    for n, (stop, *parts) in enumerate(plan):
        parts = [(arrived[packet], at) for packet, at in parts]
        add_stop(n, tiles_ref, stop(core), *parts, query_ref, sums_ref, squares_ref, stack_ref, sizes)


def more_kernel(tiles_ref, query_ref, sums_in, squares_in, *refs, plan, packets, sizes, last):
    arrived = refs[:packets]
    sums_ref, squares_ref, *stack_ref = refs[packets:]
    if last:
        payload_ref, *stack_ref = stack_ref
    add_plan(tiles_ref, plan, arrived, query_ref, sums_ref, squares_ref, stack_ref, sizes)
    if last:
        hand_out(sums_ref, squares_ref, payload_ref, sizes)


def hand_out(sums_ref, squares_ref, payload_ref, sizes):
    fibers, key_tiles, tile, scale = sizes
    rows = key_tiles * tile
    half = EXTRA_ROWS // 2
    for r in range(1, fibers):
        payload_ref[r - 1, :rows, :] = sums_ref[r * rows : (r + 1) * rows, :].astype(jnp.bfloat16)
        for t in range(key_tiles):
            den = squares_ref[r * rows + t * tile : r * rows + (t + 1) * tile, :]
            high = den.astype(jnp.bfloat16)
            rest = den - high.astype(jnp.float32)
            both = jnp.concatenate([high.astype(jnp.float32).T[:half], rest.T[:half]], axis=0)
            payload_ref[r - 1, rows : rows + EXTRA_ROWS, t * tile : (t + 1) * tile] = both.astype(jnp.bfloat16)


def finish_kernel(num_ref, den_ref, *refs, sizes):
    fibers, key_tiles, tile, scale = sizes
    *payloads, out_ref = refs
    rows, feats = out_ref.shape
    head_dim = feats // HEADS
    half = EXTRA_ROWS // 2
    head_of = lax.broadcasted_iota(jnp.int32, (tile, feats), 1) // head_dim
    for t in range(key_tiles):
        here = slice(t * tile, (t + 1) * tile)
        num = num_ref[here, :]
        den = den_ref[here, :]
        for payload in payloads:
            num = num + payload[here, :].astype(jnp.float32)
            both = payload[rows : rows + EXTRA_ROWS, here].astype(jnp.float32)
            total = both[:half] + both[half:]
            padded = jnp.concatenate([total, jnp.zeros((LANES - half, tile), jnp.float32)], axis=0)
            den = den + padded.T
        spread = lax.rsqrt(1.0 + den)
        factor = jnp.broadcast_to(spread[:, 0:1], (tile, feats))
        for h in range(1, HEADS):
            factor = jnp.where(head_of == h, spread[:, h : h + 1], factor)
        out_ref[here, :] = (num * factor).astype(jnp.bfloat16)


def on_device(queries, keys, values, tiles, edges):
    fibers = lax.axis_size("fiber")
    rows, feats = keys.shape
    stops, capacity, tile = tiles.shape[2], tiles.shape[3], edges.shape[-1]
    key_tiles = rows // tile
    scale = (feats // HEADS) ** (-0.5) * (stops * fibers * rows / 4) ** (-0.5)
    sizes = (fibers, key_tiles, tile, scale)
    half_rows = feats // LANES * rows
    list_rows = capacity * tile

    shifts = range(CORES, stops, CORES)
    far = [moved((keys, values), "blk", s) for s in shifts]
    own, odd, *pairs = packed(
        keys, values, edges,
        [
            (True, [lambda core: 0]),
            (True, [lambda core: jnp.where(core == 1, stops - 1, 1)]),
        ]
        + [(False, [lambda core, s=s: jnp.where(core == 1, s - 1, s + 1), lambda core, s=s: s]) for s in shifts],
    )
    near = [routed(block, lambda i: i ^ 1) for block in far]
    pairs = [moved(pair, "blk", s) for pair, s in zip(pairs, shifts)]
    odd = routed(odd, lambda i: i - 1 if i % CORES else i - stops + 1)
    all_queries = [queries] + [moved(queries, "fiber", -r) for r in range(1, fibers)]

    smem = pl.BlockSpec(memory_space=pltpu.SMEM)
    state = [
        jax.ShapeDtypeStruct((fibers * rows, feats), jnp.bfloat16),
        jax.ShapeDtypeStruct((fibers * rows, feats), jnp.float32),
        jax.ShapeDtypeStruct((fibers * rows, LANES), jnp.float32),
    ]

    plan = [(lambda core: 0, (0, 0), (0, half_rows), (0, 2 * half_rows))]
    all_q, sums, squares = pl.pallas_call(
        functools.partial(first_kernel, plan=plan, packets=1, sizes=sizes),
        in_specs=[smem] + [WHOLE] * (1 + fibers),
        out_specs=[WHOLE] * 3,
        out_shape=state,
        scratch_shapes=stacks(len(plan), key_tiles, tile, feats),
        compiler_params=PARAMS,
        cost_estimate=SHORT,
    )(tiles, *all_queries, own)
    pairs, near, all_q, sums, squares = lax.optimization_barrier((pairs, near, all_q, sums, squares))
    far_packets, far_plan, near_packets, near_plan = [], [], [], []
    for s, pair, far_block, near_block in zip(shifts, pairs, far, near):
        at = len(far_packets)
        far_packets += [*far_block, pair]
        near_packets += [*near_block, routed(pair[:list_rows], lambda i: i ^ 1)]
        far_plan.append((lambda core, s=s: s, (at, 0), (at + 1, 0), (at + 2, list_rows)))
        near_plan.append((lambda core, s=s: jnp.where(core == 0, s - 1, s + 1), (at, 0), (at + 1, 0), (at + 2, 0)))
    at = len(near_packets)
    near_packets.append(odd)
    near_plan.append((lambda core: jnp.where(core == 0, stops - 1, 1), (at, 0), (at, half_rows), (at, 2 * half_rows)))
    for packets, plan, last in ((far_packets, far_plan, False), (near_packets, near_plan, True)):
        sums, squares, *payload = pl.pallas_call(
            functools.partial(more_kernel, plan=plan, packets=len(packets), sizes=sizes, last=last),
            in_specs=[smem] + [WHOLE] * (3 + len(packets)),
            out_specs=[WHOLE] * (2 + last),
            out_shape=state[1:]
            + [jax.ShapeDtypeStruct((max(fibers - 1, 1), rows + EXTRA_ROWS, feats), jnp.bfloat16)] * last,
            input_output_aliases={2: 0, 3: 1},
            scratch_shapes=stacks(len(plan), key_tiles, tile, feats),
            compiler_params=PARAMS,
            cost_estimate=SHORT,
        )(tiles, all_q, sums, squares, *packets)
    [payload] = payload
    partials = [moved(payload[r - 1], "fiber", r) for r in range(1, fibers)]
    return pl.pallas_call(
        functools.partial(finish_kernel, sizes=sizes),
        in_specs=[WHOLE] * (2 + len(partials)),
        out_specs=WHOLE,
        out_shape=jax.ShapeDtypeStruct((rows, feats), jnp.bfloat16),
        compiler_params=PARAMS,
        cost_estimate=SHORT,
    )(sums, squares, *partials)


def solution(mesh):
    return jax.shard_map(
        on_device,
        mesh=mesh,
        in_specs=(
            P(("blk", "fiber"), None),
            P(("blk", "fiber"), None),
            P(("blk", "fiber"), None),
            P("blk", "fiber", None, None),
            P("blk", "fiber", None, None, None, None),
        ),
        out_specs=P(("blk", "fiber"), None),
        check_vma=False,
    )
```

```python
import functools
import math

import jax
import jax.numpy as jnp
from jax import lax
from jax.experimental import pallas as pl
from jax.experimental.pallas import tpu as pltpu
from jax.sharding import PartitionSpec as P

HEADS = 4
LEAKY_SLOPE = 0.2
CORES = 2
UNROLL = 4
EXTRA_ROWS = 16
LANES = 128
VMEM_BYTES = 32 * 2**20
WHOLE = pl.BlockSpec(memory_space=pltpu.VMEM)
ANYWHERE = pl.BlockSpec(memory_space=pltpu.HBM)
PARAMS = pltpu.CompilerParams(vmem_limit_bytes=VMEM_BYTES)
SHORT = pl.CostEstimate(flops=1, bytes_accessed=1, transcendentals=0)


def moved(block, axis, distance):
    count = lax.axis_size(axis)
    return lax.ppermute(block, axis, [((i - distance) % count, i) for i in range(count)])


def routed(block, source_of):
    count = lax.axis_size("blk")
    return lax.ppermute(block, "blk", [(source_of(i) % count, i) for i in range(count)])


def core_of_blk():
    return lax.rem(lax.axis_index("blk"), CORES)


def pack_kernel(key_ref, value_ref, edges_ref, *refs, lists):
    *outs, sem = refs
    rows, feats = key_ref.shape
    list_rows = edges_ref.shape[1]
    core = core_of_blk()
    copies = []
    for out_ref, (with_block, stops) in zip(outs, lists):
        at = 0
        if with_block:
            for ref in (key_ref, value_ref):
                for c in range(0, feats, LANES):
                    copies.append((ref.at[:, c : c + LANES], out_ref.at[at : at + rows, :]))
                    at += rows
        for stop in stops:
            copies.append((edges_ref.at[stop(core)], out_ref.at[at : at + list_rows, :]))
            at += list_rows
    running = [pltpu.make_async_copy(a, b, sem.at[n]) for n, (a, b) in enumerate(copies)]
    for copy in running:
        copy.start()
    for copy in running:
        copy.wait()


def packed(keys, values, edges, lists):
    rows, feats = keys.shape
    capacity, tile = edges.shape[3], edges.shape[4]
    block = 2 * feats // LANES
    sizes = [(block * rows if with_block else 0) + len(stops) * capacity * tile for with_block, stops in lists]
    count = sum((block if with_block else 0) + len(stops) for with_block, stops in lists)
    return pl.pallas_call(
        functools.partial(pack_kernel, lists=lists),
        in_specs=[ANYWHERE] * 3,
        out_specs=[WHOLE] * len(lists),
        out_shape=[jax.ShapeDtypeStruct((size, LANES), jnp.bfloat16) for size in sizes],
        scratch_shapes=[pltpu.SemaphoreType.DMA((count,))],
        compiler_params=PARAMS,
        cost_estimate=SHORT,
    )(*[pltpu.with_memory_space_constraint(x, pltpu.HBM) for x in (keys, values, edges.reshape(edges.shape[2], capacity * tile, tile))])


def head_masked(block, head_count):
    head_dim = block.shape[1] // head_count
    head_of = lax.broadcasted_iota(jnp.int32, block.shape, 1) // head_dim
    return jnp.concatenate(
        [jnp.where(head_of == h, block, jnp.zeros_like(block)) for h in range(head_count)], axis=0
    )


def tile_of(part, c, rows, tile, feats):
    ref, at = part
    wide = ref.shape[1]
    starts = [at + piece * rows + c * tile for piece in range(feats // wide)]
    return jnp.concatenate([ref[s : s + tile, :] for s in starts], axis=1)


def stack_keys(key_stack, at, block):
    feats, tile = block.shape[1], block.shape[0]
    turned = block.T
    head_of = lax.broadcasted_iota(jnp.int32, (feats, tile), 0) // (feats // HEADS)
    key_stack[at] = jnp.concatenate(
        [jnp.where(head_of == h, turned, jnp.zeros_like(turned)) for h in range(HEADS)], axis=1
    )


def stacks(count, key_tiles, tile, feats):
    return [
        pltpu.VMEM((count * key_tiles, feats, HEADS * tile), jnp.bfloat16),
        pltpu.VMEM((count * key_tiles, HEADS * tile, feats), jnp.bfloat16),
    ]


def entries(tiles_ref, stop, first, count, numbers):
    bits = numbers.bit_length()
    lists = tiles_ref[0, 0]
    slot = lax.broadcasted_iota(jnp.int32, lists.shape, 1) - first
    here = (lax.broadcasted_iota(jnp.int32, lists.shape, 0) == stop) & (slot >= 0) & (slot < count)
    shift = jnp.where(here, slot * bits, 0)
    together = jnp.sum(jnp.where(here, lax.shift_left(lists + 1, shift), 0))
    return [(lax.shift_right_logical(together, k * bits) & ((1 << bits) - 1)) - 1 for k in range(count)]


def place_of(listed, key_tiles, tile, fibers):
    number = jnp.maximum(listed, 0)
    row_tile = lax.div(number, key_tiles)
    part = lax.rem(lax.div(row_tile, key_tiles) - lax.axis_index("fiber") + fibers, fibers)
    at = pl.multiple_of((part * key_tiles + lax.rem(row_tile, key_tiles)) * tile, tile)
    return at, lax.rem(number, key_tiles)


def over_slots(tiles_ref, stop, sizes, one_slot):
    fibers, key_tiles, tile, scale = sizes
    capacity = tiles_ref.shape[-1]
    group = math.gcd(capacity, UNROLL)

    def one_group(g, carry):
        listed = entries(tiles_ref, stop, g * group, group, fibers * key_tiles * key_tiles)
        for k in range(group):
            one_slot(g * group + k, listed[k])
        return carry

    if capacity == group:
        one_group(0, 0)
    else:
        lax.fori_loop(0, capacity // group, one_group, 0)


def rows_of(first, slot, tile):
    at = first + slot * tile
    return pl.ds(at if isinstance(at, int) else pl.multiple_of(at, tile), tile)


def stack_block(first, keys, values, key_stack, value_stack, sizes):
    fibers, key_tiles, tile, scale = sizes
    feats = value_stack.shape[2]
    for c in range(key_tiles):
        stack_keys(key_stack, first + c, tile_of(keys, c, key_tiles * tile, tile, feats))
        value_stack[first + c] = head_masked(tile_of(values, c, key_tiles * tile, tile, feats), HEADS)


def bent_scores(query_ref, at, key_stack):
    scores = jnp.dot(query_ref[pl.ds(at, tile_rows(key_stack)), :], key_stack, preferred_element_type=jnp.float32)
    return jnp.maximum(scores, LEAKY_SLOPE * scores)


def tile_rows(key_stack):
    return key_stack.shape[1] // HEADS


def add_tile(bent, listed, at, edge, value_stack, sums_ref, squares_ref, scale):
    tile = edge.shape[0]
    lane = lax.broadcasted_iota(jnp.int32, (tile, LANES), 1)
    edge = jnp.where(listed >= 0, edge.astype(jnp.float32) * scale, 0.0)
    weights = bent * jnp.concatenate([edge] * HEADS, axis=1)
    squared = weights * weights
    den = jnp.zeros((tile, LANES), jnp.float32)
    for h in range(HEADS):
        total = jnp.sum(squared[:, h * tile : (h + 1) * tile], axis=1, keepdims=True)
        den = jnp.where(lane == h, total, den)
    squares_ref[pl.ds(at, tile), :] += den
    sums_ref[pl.ds(at, tile), :] += jnp.dot(weights.astype(jnp.bfloat16), value_stack, preferred_element_type=jnp.float32)


def add_plan(tiles_ref, plan, arrived, query_ref, sums_ref, squares_ref, stacks_, sizes):
    fibers, key_tiles, tile, scale = sizes
    key_stack, value_stack = stacks_
    core = core_of_blk()
    for n, (stop, *parts) in enumerate(plan):
        keys, values, (edge_ref, edge_at) = [(arrived[packet], at) for packet, at in parts]
        stack_block(n * key_tiles, keys, values, key_stack, value_stack, sizes)

        def one_slot(slot, listed, n=n, edge_ref=edge_ref, edge_at=edge_at):
            at, column = place_of(listed, key_tiles, tile, fibers)
            bent = bent_scores(query_ref, at, key_stack[n * key_tiles + column])
            edge = edge_ref[rows_of(edge_at, slot, tile), :]
            add_tile(bent, listed, at, edge, value_stack[n * key_tiles + column], sums_ref, squares_ref, scale)

        over_slots(tiles_ref, stop(core), sizes, one_slot)


def ready_kernel(tiles_ref, query_ref, *refs, plan, packets, sizes):
    fibers, key_tiles, tile, scale = sizes
    arrived, (bent_ref, value_stack, key_stack) = refs[:packets], refs[packets:]
    capacity = tiles_ref.shape[-1]
    core = core_of_blk()
    for n, (stop, *parts) in enumerate(plan):
        keys, values = [(arrived[packet], at) for packet, at in parts]
        stack_block(n * key_tiles, keys, values, key_stack, value_stack, sizes)

        def one_slot(slot, listed, n=n):
            at, column = place_of(listed, key_tiles, tile, fibers)
            bent_ref[rows_of(n * capacity * tile, slot, tile), :] = bent_scores(
                query_ref, at, key_stack[n * key_tiles + column]
            )

        over_slots(tiles_ref, stop(core), sizes, one_slot)


def edge_kernel(tiles_ref, bent_ref, value_stack, sums_in, squares_in, *refs, plan, packets, sizes, last):
    fibers, key_tiles, tile, scale = sizes
    arrived, (sums_ref, squares_ref, *payload_ref) = refs[:packets], refs[packets:]
    capacity = tiles_ref.shape[-1]
    core = core_of_blk()
    for stop, n, (packet, edge_at) in plan:

        def one_slot(slot, listed, n=n, edge_ref=arrived[packet], edge_at=edge_at):
            at, column = place_of(listed, key_tiles, tile, fibers)
            bent = bent_ref[rows_of(n * capacity * tile, slot, tile), :]
            edge = edge_ref[rows_of(edge_at, slot, tile), :]
            add_tile(bent, listed, at, edge, value_stack[n * key_tiles + column], sums_ref, squares_ref, scale)

        over_slots(tiles_ref, stop(core), sizes, one_slot)
    if last:
        hand_out(sums_ref, squares_ref, payload_ref[0], sizes)


def first_kernel(tiles_ref, *refs, plan, packets, sizes):
    fibers, key_tiles, tile, scale = sizes
    queries, arrived = refs[:fibers], refs[fibers : fibers + packets]
    query_ref, sums_ref, squares_ref, *stack_ref = refs[fibers + packets :]
    rows = key_tiles * tile
    for r in range(fibers):
        query_ref[r * rows : (r + 1) * rows, :] = queries[r][...]
    sums_ref[...] = jnp.zeros_like(sums_ref)
    squares_ref[...] = jnp.zeros_like(squares_ref)
    add_plan(tiles_ref, plan, arrived, query_ref, sums_ref, squares_ref, stack_ref, sizes)


def more_kernel(tiles_ref, query_ref, sums_in, squares_in, *refs, plan, packets, sizes):
    sums_ref, squares_ref, *stack_ref = refs[packets:]
    add_plan(tiles_ref, plan, refs[:packets], query_ref, sums_ref, squares_ref, stack_ref, sizes)


def hand_out(sums_ref, squares_ref, payload_ref, sizes):
    fibers, key_tiles, tile, scale = sizes
    rows = key_tiles * tile
    half = EXTRA_ROWS // 2
    for r in range(1, fibers):
        payload_ref[r - 1, :rows, :] = sums_ref[r * rows : (r + 1) * rows, :].astype(jnp.bfloat16)
        for t in range(key_tiles):
            den = squares_ref[r * rows + t * tile : r * rows + (t + 1) * tile, :].T[:half]
            high = den.astype(jnp.bfloat16).astype(jnp.float32)
            both = jnp.concatenate([high, den - high], axis=0)
            payload_ref[r - 1, rows : rows + EXTRA_ROWS, t * tile : (t + 1) * tile] = both.astype(jnp.bfloat16)


def finish_kernel(num_ref, den_ref, *refs, sizes):
    fibers, key_tiles, tile, scale = sizes
    *payloads, out_ref = refs
    rows, feats = out_ref.shape
    head_dim = feats // HEADS
    half = EXTRA_ROWS // 2
    head_of = lax.broadcasted_iota(jnp.int32, (tile, feats), 1) // head_dim
    for t in range(key_tiles):
        here = slice(t * tile, (t + 1) * tile)
        num = num_ref[here, :]
        den = den_ref[here, :]
        for payload in payloads:
            num = num + payload[here, :].astype(jnp.float32)
            both = payload[rows : rows + EXTRA_ROWS, here].astype(jnp.float32)
            total = both[:half] + both[half:]
            padded = jnp.concatenate([total, jnp.zeros((LANES - half, tile), jnp.float32)], axis=0)
            den = den + padded.T
        spread = lax.rsqrt(1.0 + den)
        factor = jnp.broadcast_to(spread[:, 0:1], (tile, feats))
        for h in range(1, HEADS):
            factor = jnp.where(head_of == h, spread[:, h : h + 1], factor)
        out_ref[here, :] = (num * factor).astype(jnp.bfloat16)


def on_device(queries, keys, values, tiles, edges):
    fibers = lax.axis_size("fiber")
    rows, feats = keys.shape
    stops, capacity, tile = tiles.shape[2], tiles.shape[3], edges.shape[-1]
    key_tiles = rows // tile
    scale = (feats // HEADS) ** (-0.5) * (stops * fibers * rows / 4) ** (-0.5)
    sizes = (fibers, key_tiles, tile, scale)
    half_rows = feats // LANES * rows
    list_rows = capacity * tile

    shifts = range(CORES, stops, CORES)
    far = [moved((keys, values), "blk", s) for s in shifts]
    own, odd, *pairs = packed(
        keys, values, edges,
        [
            (True, [lambda core: 0]),
            (True, [lambda core: jnp.where(core == 1, stops - 1, 1)]),
        ]
        + [(False, [lambda core, s=s: jnp.where(core == 1, s - 1, s + 1), lambda core, s=s: s]) for s in shifts],
    )
    near = [routed(block, lambda i: i ^ 1) for block in far]
    pairs = [moved(pair, "blk", s) for pair, s in zip(pairs, shifts)]
    odd = routed(odd, lambda i: i - 1 if i % CORES else i - stops + 1)
    all_queries = [queries] + [moved(queries, "fiber", -r) for r in range(1, fibers)]

    state = [
        jax.ShapeDtypeStruct((fibers * rows, feats), jnp.bfloat16),
        jax.ShapeDtypeStruct((fibers * rows, feats), jnp.float32),
        jax.ShapeDtypeStruct((fibers * rows, LANES), jnp.float32),
    ]

    plan = [(lambda core: 0, (0, 0), (0, half_rows), (0, 2 * half_rows))]
    all_q, sums, squares = pl.pallas_call(
        functools.partial(first_kernel, plan=plan, packets=1, sizes=sizes),
        in_specs=[WHOLE] * (2 + fibers),
        out_specs=[WHOLE] * 3,
        out_shape=state,
        scratch_shapes=stacks(len(plan), key_tiles, tile, feats),
        compiler_params=PARAMS,
        cost_estimate=SHORT,
    )(tiles, *all_queries, own)
    ready_packets, ready_plan, far_plan, near_plan, cross = [], [], [], [], []
    for n, (s, far_block, near_block) in enumerate(zip(shifts, far, near)):
        of_far = lambda core, s=s: s
        of_near = lambda core, s=s: jnp.where(core == 0, s - 1, s + 1)
        ready_packets += [*far_block, *near_block]
        ready_plan += [(of_far, (4 * n, 0), (4 * n + 1, 0)), (of_near, (4 * n + 2, 0), (4 * n + 3, 0))]
        far_plan.append((of_far, 2 * n, (n, list_rows)))
        near_plan.append((of_near, 2 * n + 1, (n, 0)))
    lists_ready = len(ready_plan)
    bent, value_stack = pl.pallas_call(
        functools.partial(ready_kernel, plan=ready_plan, packets=len(ready_packets), sizes=sizes),
        in_specs=[WHOLE] * (2 + len(ready_packets)),
        out_specs=[WHOLE] * 2,
        out_shape=[
            jax.ShapeDtypeStruct((lists_ready * list_rows, HEADS * tile), jnp.float32),
            jax.ShapeDtypeStruct((lists_ready * key_tiles, HEADS * tile, feats), jnp.bfloat16),
        ],
        scratch_shapes=stacks(lists_ready, key_tiles, tile, feats)[:1],
        compiler_params=PARAMS,
        cost_estimate=SHORT,
    )(tiles, all_q, *ready_packets)
    pairs, bent, value_stack, sums, squares = lax.optimization_barrier((pairs, bent, value_stack, sums, squares))
    cross = [routed(pair[:list_rows], lambda i: i ^ 1) for pair in pairs]

    def add_edges(packets, plan, sums, squares, last):
        return pl.pallas_call(
            functools.partial(edge_kernel, plan=plan, packets=len(packets), sizes=sizes, last=last),
            in_specs=[WHOLE] * (5 + len(packets)),
            out_specs=[WHOLE] * (2 + last),
            out_shape=state[1:]
            + [jax.ShapeDtypeStruct((max(fibers - 1, 1), rows + EXTRA_ROWS, feats), jnp.bfloat16)] * last,
            input_output_aliases={3: 0, 4: 1},
            compiler_params=PARAMS,
            cost_estimate=SHORT,
        )(tiles, bent, value_stack, sums, squares, *packets)

    sums, squares = add_edges(pairs, far_plan, sums, squares, False)
    odd_plan = [(lambda core: jnp.where(core == 0, stops - 1, 1), (0, 0), (0, half_rows), (0, 2 * half_rows))]
    sums, squares = pl.pallas_call(
        functools.partial(more_kernel, plan=odd_plan, packets=1, sizes=sizes),
        in_specs=[WHOLE] * 5,
        out_specs=[WHOLE] * 2,
        out_shape=state[1:],
        input_output_aliases={2: 0, 3: 1},
        scratch_shapes=stacks(1, key_tiles, tile, feats),
        compiler_params=PARAMS,
        cost_estimate=SHORT,
    )(tiles, all_q, sums, squares, odd)
    sums, squares, payload = add_edges(cross, near_plan, sums, squares, True)
    partials = [moved(payload[r - 1], "fiber", r) for r in range(1, fibers)]
    return pl.pallas_call(
        functools.partial(finish_kernel, sizes=sizes),
        in_specs=[WHOLE] * (2 + len(partials)),
        out_specs=WHOLE,
        out_shape=jax.ShapeDtypeStruct((rows, feats), jnp.bfloat16),
        compiler_params=PARAMS,
        cost_estimate=SHORT,
    )(sums, squares, *partials)


def solution(mesh):
    return jax.shard_map(
        on_device,
        mesh=mesh,
        in_specs=(
            P(("blk", "fiber"), None),
            P(("blk", "fiber"), None),
            P(("blk", "fiber"), None),
            P("blk", "fiber", None, None),
            P("blk", "fiber", None, None, None, None),
        ),
        out_specs=P(("blk", "fiber"), None),
        check_vma=False,
    )
```

```python
import functools
import math

import jax
import jax.numpy as jnp
from jax import lax
from jax.experimental import pallas as pl
from jax.experimental.pallas import tpu as pltpu
from jax.sharding import PartitionSpec as P

HEADS = 4
LEAKY_SLOPE = 0.2
CORES = 2
UNROLL = 4
EXTRA_ROWS = 16
LANES = 128
VMEM_BYTES = 32 * 2**20
WHOLE = pl.BlockSpec(memory_space=pltpu.VMEM)
ANYWHERE = pl.BlockSpec(memory_space=pltpu.HBM)
PARAMS = pltpu.CompilerParams(vmem_limit_bytes=VMEM_BYTES)
SHORT = pl.CostEstimate(flops=1, bytes_accessed=1, transcendentals=0)


def moved(block, axis, distance):
    count = lax.axis_size(axis)
    return lax.ppermute(block, axis, [((i - distance) % count, i) for i in range(count)])


def routed(block, source_of):
    count = lax.axis_size("blk")
    return lax.ppermute(block, "blk", [(source_of(i) % count, i) for i in range(count)])


def core_of_blk():
    return lax.rem(lax.axis_index("blk"), CORES)


def pack_kernel(key_ref, value_ref, edges_ref, *refs, lists):
    *outs, sem = refs
    rows, feats = key_ref.shape
    list_rows = edges_ref.shape[1]
    core = core_of_blk()
    copies = []
    for out_ref, (with_block, stops) in zip(outs, lists):
        at = 0
        if with_block:
            for ref in (key_ref, value_ref):
                for c in range(0, feats, LANES):
                    copies.append((ref.at[:, c : c + LANES], out_ref.at[at : at + rows, :]))
                    at += rows
        for stop in stops:
            copies.append((edges_ref.at[stop(core)], out_ref.at[at : at + list_rows, :]))
            at += list_rows
    running = [pltpu.make_async_copy(a, b, sem.at[n]) for n, (a, b) in enumerate(copies)]
    for copy in running:
        copy.start()
    for copy in running:
        copy.wait()


def packed(keys, values, edges, lists):
    rows, feats = keys.shape
    capacity, tile = edges.shape[3], edges.shape[4]
    block = 2 * feats // LANES
    sizes = [(block * rows if with_block else 0) + len(stops) * capacity * tile for with_block, stops in lists]
    count = sum((block if with_block else 0) + len(stops) for with_block, stops in lists)
    return pl.pallas_call(
        functools.partial(pack_kernel, lists=lists),
        in_specs=[ANYWHERE] * 3,
        out_specs=[WHOLE] * len(lists),
        out_shape=[jax.ShapeDtypeStruct((size, LANES), jnp.bfloat16) for size in sizes],
        scratch_shapes=[pltpu.SemaphoreType.DMA((count,))],
        compiler_params=PARAMS,
        cost_estimate=SHORT,
    )(*[pltpu.with_memory_space_constraint(x, pltpu.HBM) for x in (keys, values, edges.reshape(edges.shape[2], capacity * tile, tile))])


def head_masked(block, head_count):
    head_dim = block.shape[1] // head_count
    head_of = lax.broadcasted_iota(jnp.int32, block.shape, 1) // head_dim
    return jnp.concatenate(
        [jnp.where(head_of == h, block, jnp.zeros_like(block)) for h in range(head_count)], axis=0
    )


def tile_of(part, c, rows, tile, feats):
    ref, at = part
    wide = ref.shape[1]
    starts = [at + piece * rows + c * tile for piece in range(feats // wide)]
    return jnp.concatenate([ref[s : s + tile, :] for s in starts], axis=1)


def stack_keys(key_stack, at, block):
    feats, tile = block.shape[1], block.shape[0]
    turned = block.T
    head_of = lax.broadcasted_iota(jnp.int32, (feats, tile), 0) // (feats // HEADS)
    key_stack[at] = jnp.concatenate(
        [jnp.where(head_of == h, turned, jnp.zeros_like(turned)) for h in range(HEADS)], axis=1
    )


def stacks(count, key_tiles, tile, feats):
    return [
        pltpu.VMEM((count * key_tiles, feats, HEADS * tile), jnp.bfloat16),
        pltpu.VMEM((count * key_tiles, HEADS * tile, feats), jnp.bfloat16),
    ]


def entries(tiles_ref, stop, first, count, numbers):
    bits = numbers.bit_length()
    lists = tiles_ref[0, 0]
    slot = lax.broadcasted_iota(jnp.int32, lists.shape, 1) - first
    here = (lax.broadcasted_iota(jnp.int32, lists.shape, 0) == stop) & (slot >= 0) & (slot < count)
    shift = jnp.where(here, slot * bits, 0)
    together = jnp.sum(jnp.where(here, lax.shift_left(lists + 1, shift), 0))
    return [(lax.shift_right_logical(together, k * bits) & ((1 << bits) - 1)) - 1 for k in range(count)]


def place_of(listed, key_tiles, tile, fibers):
    number = jnp.maximum(listed, 0)
    row_tile = lax.div(number, key_tiles)
    part = lax.rem(lax.div(row_tile, key_tiles) - lax.axis_index("fiber") + fibers, fibers)
    at = pl.multiple_of((part * key_tiles + lax.rem(row_tile, key_tiles)) * tile, tile)
    return at, lax.rem(number, key_tiles)


def over_groups(tiles_ref, stop, sizes, one_group):
    fibers, key_tiles, tile, scale = sizes
    capacity = tiles_ref.shape[-1]
    group = math.gcd(capacity, UNROLL)

    def step(g, carry):
        first = g * group
        one_group(first, entries(tiles_ref, stop, first, group, fibers * key_tiles * key_tiles))
        return carry

    if capacity == group:
        step(0, 0)
    else:
        lax.fori_loop(0, capacity // group, step, 0)


def rows_of(first, slot, tile):
    at = first + slot * tile
    return pl.ds(at if isinstance(at, int) else pl.multiple_of(at, tile), tile)


def stack_block(first, keys, values, key_stack, value_stack, sizes):
    fibers, key_tiles, tile, scale = sizes
    feats = value_stack.shape[2]
    for c in range(key_tiles):
        stack_keys(key_stack, first + c, tile_of(keys, c, key_tiles * tile, tile, feats))
        value_stack[first + c] = head_masked(tile_of(values, c, key_tiles * tile, tile, feats), HEADS)


def bent_scores(query_ref, at, key_stack):
    scores = jnp.dot(query_ref[pl.ds(at, tile_rows(key_stack)), :], key_stack, preferred_element_type=jnp.float32)
    return jnp.maximum(scores, LEAKY_SLOPE * scores)


def tile_rows(key_stack):
    return key_stack.shape[1] // HEADS


def blended(bent, edge, value_stack, scale):
    tile = edge.shape[0]
    lane = lax.broadcasted_iota(jnp.int32, (tile, LANES), 1)
    edge = edge.astype(jnp.float32) * scale
    weights = bent * jnp.concatenate([edge] * HEADS, axis=1)
    squared = weights * weights
    den = jnp.zeros((tile, LANES), jnp.float32)
    for h in range(HEADS):
        total = jnp.sum(squared[:, h * tile : (h + 1) * tile], axis=1, keepdims=True)
        den = jnp.where(lane == h, total, den)
    return jnp.dot(weights.astype(jnp.bfloat16), value_stack, preferred_element_type=jnp.float32), den


def add_plan(tiles_ref, plan, arrived, query_ref, sums_ref, squares_ref, stacks_, sizes):
    fibers, key_tiles, tile, scale = sizes
    key_stack, value_stack = stacks_
    core = core_of_blk()
    for n, (stop, *parts) in enumerate(plan):
        keys, values, (edge_ref, edge_at) = [(arrived[packet], at) for packet, at in parts]
        capacity = tiles_ref.shape[-1]

        def one_group(first, listed, n=n, edge_ref=edge_ref, edge_at=edge_at):
            for k, number in enumerate(listed):
                at, column = place_of(number, key_tiles, tile, fibers)
                bent = bent_scores(query_ref, at, key_stack[n * key_tiles + column])
                bent = jnp.where(number >= 0, bent, 0.0)
                edge = edge_ref[rows_of(edge_at, first + k, tile), :]
                num, den = blended(bent, edge, value_stack[n * key_tiles + column], scale)
                squares_ref[pl.ds(at, tile), :] += den
                sums_ref[pl.ds(at, tile), :] += num

        stack_block(n * key_tiles, keys, values, key_stack, value_stack, sizes)
        over_groups(tiles_ref, stop(core), sizes, one_group)


def ready_kernel(tiles_ref, query_ref, *refs, plan, packets, sizes):
    fibers, key_tiles, tile, scale = sizes
    arrived, (bent_ref, slot_values, key_stack, value_stack) = refs[:packets], refs[packets:]
    capacity = tiles_ref.shape[-1]
    core = core_of_blk()
    for n, (stop, *parts) in enumerate(plan):
        keys, values = [(arrived[packet], at) for packet, at in parts]
        stack_block(n * key_tiles, keys, values, key_stack, value_stack, sizes)

        def one_group(first, listed, n=n):
            for k, number in enumerate(listed):
                at, column = place_of(number, key_tiles, tile, fibers)
                bent = bent_scores(query_ref, at, key_stack[n * key_tiles + column])
                bent_ref[rows_of(n * capacity * tile, first + k, tile), :] = jnp.where(number >= 0, bent, 0.0)
                slot_values[n * capacity + first + k] = value_stack[n * key_tiles + column]

        over_groups(tiles_ref, stop(core), sizes, one_group)


def edge_kernel(tiles_ref, bent_ref, slot_values, sums_in, squares_in, *refs, plan, packets, sizes, last):
    fibers, key_tiles, tile, scale = sizes
    arrived, (sums_ref, squares_ref, *payload_ref, num_ref, den_ref) = refs[:packets], refs[packets:]
    capacity = tiles_ref.shape[-1]
    core = core_of_blk()
    for stop, n, (packet, edge_at) in plan:

        def one_group(first, listed, n=n, edge_ref=arrived[packet], edge_at=edge_at):
            for k in range(len(listed)):
                bent = bent_ref[rows_of(n * capacity * tile, first + k, tile), :]
                edge = edge_ref[rows_of(edge_at, first + k, tile), :]
                num_ref[n, k], den_ref[n, k] = blended(bent, edge, slot_values[n * capacity + first + k], scale)
            for k, number in enumerate(listed):
                at, _ = place_of(number, key_tiles, tile, fibers)
                squares_ref[pl.ds(at, tile), :] += den_ref[n, k]
                sums_ref[pl.ds(at, tile), :] += num_ref[n, k]

        over_groups(tiles_ref, stop(core), sizes, one_group)
    if last:
        hand_out(sums_ref, squares_ref, payload_ref[0], sizes)


def first_kernel(tiles_ref, *refs, plan, packets, sizes):
    fibers, key_tiles, tile, scale = sizes
    queries, arrived = refs[:fibers], refs[fibers : fibers + packets]
    query_ref, sums_ref, squares_ref, *stack_ref = refs[fibers + packets :]
    rows = key_tiles * tile
    for r in range(fibers):
        query_ref[r * rows : (r + 1) * rows, :] = queries[r][...]
    sums_ref[...] = jnp.zeros_like(sums_ref)
    squares_ref[...] = jnp.zeros_like(squares_ref)
    add_plan(tiles_ref, plan, arrived, query_ref, sums_ref, squares_ref, stack_ref, sizes)


def more_kernel(tiles_ref, query_ref, sums_in, squares_in, *refs, plan, packets, sizes):
    sums_ref, squares_ref, *stack_ref = refs[packets:]
    add_plan(tiles_ref, plan, refs[:packets], query_ref, sums_ref, squares_ref, stack_ref, sizes)


def hand_out(sums_ref, squares_ref, payload_ref, sizes):
    fibers, key_tiles, tile, scale = sizes
    rows = key_tiles * tile
    half = EXTRA_ROWS // 2
    for r in range(1, fibers):
        payload_ref[r - 1, :rows, :] = sums_ref[r * rows : (r + 1) * rows, :].astype(jnp.bfloat16)
        for t in range(key_tiles):
            den = squares_ref[r * rows + t * tile : r * rows + (t + 1) * tile, :].T[:half]
            high = den.astype(jnp.bfloat16).astype(jnp.float32)
            both = jnp.concatenate([high, den - high], axis=0)
            payload_ref[r - 1, rows : rows + EXTRA_ROWS, t * tile : (t + 1) * tile] = both.astype(jnp.bfloat16)


def finish_kernel(num_ref, den_ref, *refs, sizes):
    fibers, key_tiles, tile, scale = sizes
    *payloads, out_ref = refs
    rows, feats = out_ref.shape
    head_dim = feats // HEADS
    half = EXTRA_ROWS // 2
    head_of = lax.broadcasted_iota(jnp.int32, (tile, feats), 1) // head_dim
    for t in range(key_tiles):
        here = slice(t * tile, (t + 1) * tile)
        num = num_ref[here, :]
        den = den_ref[here, :]
        for payload in payloads:
            num = num + payload[here, :].astype(jnp.float32)
            both = payload[rows : rows + EXTRA_ROWS, here].astype(jnp.float32)
            total = both[:half] + both[half:]
            padded = jnp.concatenate([total, jnp.zeros((LANES - half, tile), jnp.float32)], axis=0)
            den = den + padded.T
        spread = lax.rsqrt(1.0 + den)
        factor = jnp.broadcast_to(spread[:, 0:1], (tile, feats))
        for h in range(1, HEADS):
            factor = jnp.where(head_of == h, spread[:, h : h + 1], factor)
        out_ref[here, :] = (num * factor).astype(jnp.bfloat16)


def on_device(queries, keys, values, tiles, edges):
    fibers = lax.axis_size("fiber")
    rows, feats = keys.shape
    stops, capacity, tile = tiles.shape[2], tiles.shape[3], edges.shape[-1]
    key_tiles = rows // tile
    scale = (feats // HEADS) ** (-0.5) * (stops * fibers * rows / 4) ** (-0.5)
    sizes = (fibers, key_tiles, tile, scale)
    half_rows = feats // LANES * rows
    list_rows = capacity * tile

    shifts = range(CORES, stops, CORES)
    far = [moved((keys, values), "blk", s) for s in shifts]
    own, odd, *pairs = packed(
        keys, values, edges,
        [
            (True, [lambda core: 0]),
            (True, [lambda core: jnp.where(core == 1, stops - 1, 1)]),
        ]
        + [(False, [lambda core, s=s: jnp.where(core == 1, s - 1, s + 1), lambda core, s=s: s]) for s in shifts],
    )
    near = [routed(block, lambda i: i ^ 1) for block in far]
    pairs = [moved(pair, "blk", s) for pair, s in zip(pairs, shifts)]
    odd = routed(odd, lambda i: i - 1 if i % CORES else i - stops + 1)
    all_queries = [queries] + [moved(queries, "fiber", -r) for r in range(1, fibers)]

    state = [
        jax.ShapeDtypeStruct((fibers * rows, feats), jnp.bfloat16),
        jax.ShapeDtypeStruct((fibers * rows, feats), jnp.float32),
        jax.ShapeDtypeStruct((fibers * rows, LANES), jnp.float32),
    ]

    plan = [(lambda core: 0, (0, 0), (0, half_rows), (0, 2 * half_rows))]
    all_q, sums, squares = pl.pallas_call(
        functools.partial(first_kernel, plan=plan, packets=1, sizes=sizes),
        in_specs=[WHOLE] * (2 + fibers),
        out_specs=[WHOLE] * 3,
        out_shape=state,
        scratch_shapes=stacks(len(plan), key_tiles, tile, feats),
        compiler_params=PARAMS,
        cost_estimate=SHORT,
    )(tiles, *all_queries, own)
    ready_packets, ready_plan, far_plan, near_plan, cross = [], [], [], [], []
    for n, (s, far_block, near_block) in enumerate(zip(shifts, far, near)):
        of_far = lambda core, s=s: s
        of_near = lambda core, s=s: jnp.where(core == 0, s - 1, s + 1)
        ready_packets += [*far_block, *near_block]
        ready_plan += [(of_far, (4 * n, 0), (4 * n + 1, 0)), (of_near, (4 * n + 2, 0), (4 * n + 3, 0))]
        far_plan.append((of_far, 2 * n, (n, list_rows)))
        near_plan.append((of_near, 2 * n + 1, (n, 0)))
    lists_ready = len(ready_plan)
    bent, slot_values = pl.pallas_call(
        functools.partial(ready_kernel, plan=ready_plan, packets=len(ready_packets), sizes=sizes),
        in_specs=[WHOLE] * (2 + len(ready_packets)),
        out_specs=[WHOLE] * 2,
        out_shape=[
            jax.ShapeDtypeStruct((lists_ready * list_rows, HEADS * tile), jnp.float32),
            jax.ShapeDtypeStruct((lists_ready * capacity, HEADS * tile, feats), jnp.bfloat16),
        ],
        scratch_shapes=stacks(lists_ready, key_tiles, tile, feats),
        compiler_params=PARAMS,
        cost_estimate=SHORT,
    )(tiles, all_q, *ready_packets)
    pairs, bent, slot_values, sums, squares = lax.optimization_barrier((pairs, bent, slot_values, sums, squares))
    cross = [routed(pair[:list_rows], lambda i: i ^ 1) for pair in pairs]

    def add_edges(packets, plan, sums, squares, last):
        return pl.pallas_call(
            functools.partial(edge_kernel, plan=plan, packets=len(packets), sizes=sizes, last=last),
            in_specs=[WHOLE] * (5 + len(packets)),
            out_specs=[WHOLE] * (2 + last),
            out_shape=state[1:]
            + [jax.ShapeDtypeStruct((max(fibers - 1, 1), rows + EXTRA_ROWS, feats), jnp.bfloat16)] * last,
            input_output_aliases={3: 0, 4: 1},
            scratch_shapes=[
                pltpu.VMEM((lists_ready, math.gcd(capacity, UNROLL), tile, width), jnp.float32) for width in (feats, LANES)
            ],
            compiler_params=PARAMS,
            cost_estimate=SHORT,
        )(tiles, bent, slot_values, sums, squares, *packets)

    sums, squares = add_edges(pairs, far_plan, sums, squares, False)
    odd_plan = [(lambda core: jnp.where(core == 0, stops - 1, 1), (0, 0), (0, half_rows), (0, 2 * half_rows))]
    sums, squares = pl.pallas_call(
        functools.partial(more_kernel, plan=odd_plan, packets=1, sizes=sizes),
        in_specs=[WHOLE] * 5,
        out_specs=[WHOLE] * 2,
        out_shape=state[1:],
        input_output_aliases={2: 0, 3: 1},
        scratch_shapes=stacks(1, key_tiles, tile, feats),
        compiler_params=PARAMS,
        cost_estimate=SHORT,
    )(tiles, all_q, sums, squares, odd)
    sums, squares, payload = add_edges(cross, near_plan, sums, squares, True)
    partials = [moved(payload[r - 1], "fiber", r) for r in range(1, fibers)]
    return pl.pallas_call(
        functools.partial(finish_kernel, sizes=sizes),
        in_specs=[WHOLE] * (2 + len(partials)),
        out_specs=WHOLE,
        out_shape=jax.ShapeDtypeStruct((rows, feats), jnp.bfloat16),
        compiler_params=PARAMS,
        cost_estimate=SHORT,
    )(sums, squares, *partials)


def solution(mesh):
    return jax.shard_map(
        on_device,
        mesh=mesh,
        in_specs=(
            P(("blk", "fiber"), None),
            P(("blk", "fiber"), None),
            P(("blk", "fiber"), None),
            P("blk", "fiber", None, None),
            P("blk", "fiber", None, None, None, None),
        ),
        out_specs=P(("blk", "fiber"), None),
        check_vma=False,
    )
```
